32 devices in a mesh: ax: 4 (over x, core), circ: 8 (over z, y).
Axes of the slice: x: 2, y: 2, z: 4, core: 2. Of those that a mesh axis runs over, the one named last changes fastest.
Arguments:
- load: float32 [32, 256, 3, 192], P('ax', 'circ'), may hold values from -6 to 6
- region: int32 [32, 256, 192], P('ax', 'circ'), may hold values from 0 to 1
- family: int32 [32, 256, 192], P('ax', 'circ'), may hold values from 0 to 1, as said below
- stiffness: float32 [2, 3], replicated, may hold values from 1 to 4
- coupling: float32 [2, 3, 3], replicated, may hold values from -0.6 to 0.6
- line_inverse: float32 [3, 3, 192, 192], replicated, may hold values from 0 to 1
- axial_inverse: float32 [8, 8], replicated, may hold values from 0 to 2
Outputs:
- solution: float32 [32, 256, 3, 192], P('ax', 'circ')
- residual: float32 [32, 256, 3, 192], P('ax', 'circ')
- coarse_iterate: float32 [8, 256, 3, 192], P('ax', 'circ')
The draws below stay inside these ranges and needn't reach their ends.
Inputs may be any that keep to these rules, and one draw needn't show every extreme that they name: family is 0 or 1 per cell.
All inputs are finite; a program needn't handle non-finite values.
Results may differ from the reference program's by a relative error of at most 0.0003.
Values sent between devices are 32-bit elements; how exact they have to be, the bound alone decides.
A program may use at most 128 MiB of HBM per device.

```python
import math
import jax
import jax.numpy as jnp
from jax import lax

CA = 8
R = 192
NA = 32
NC = 256


def draw_family(key, part):
    keys = jax.random.split(jax.random.fold_in(key, 11), 2)
    level = jax.random.randint(keys[0], (NA // CA, 1, 1), 0, 101)
    level = jnp.repeat(level, CA, axis=0)
    cells = jax.random.randint(keys[1], (NA, NC, R), 0, 100)
    return (cells < level).astype(jnp.int32)


def draw_line_inverse(key, part):
    keys = jax.random.split(key, 3)
    level_weight = jnp.array([1.0, 0.25, 0.0625], jnp.float32)[:, None]
    excess = (2.0 * level_weight + 2.5) / 1024.0 * jax.random.uniform(keys[0], (3, 3), jnp.float32, 0.8, 1.2)
    half = 0.5 * excess
    theta = jnp.log1p(half + jnp.sqrt(half * (2.0 + half)))[:, :, None, None]
    divisor = 1024.0 * jax.random.uniform(keys[1], (3, 3), jnp.float32, 4.0, 6.0)
    rows = jnp.arange(1, R + 1, dtype=jnp.float32)[:, None]
    cols = jnp.arange(1, R + 1, dtype=jnp.float32)[None, :]
    lower = jnp.minimum(rows, cols)[None, None]
    higher = jnp.maximum(rows, cols)[None, None]
    ends = R + 1.0
    top = jnp.exp((lower - higher - 1.0) * theta) * (1.0 - jnp.exp(-2.0 * lower * theta)) * (1.0 - jnp.exp(-2.0 * (ends - higher) * theta))
    bottom = (1.0 - jnp.exp(-2.0 * theta)) * (1.0 - jnp.exp(-2.0 * ends * theta))
    noise = 1.0 + 0.05 * jax.random.uniform(keys[2], (3, 3, R, R), jnp.float32, -1.0, 1.0)
    return (top / bottom / divisor[:, :, None, None] * noise).astype(jnp.float32)


def draw_axial_inverse(key, part):
    count = NA // 4
    keys = jax.random.split(jax.random.fold_in(key, 7), 2)
    rows = jnp.arange(count, dtype=jnp.float32)[:, None]
    cols = jnp.arange(count, dtype=jnp.float32)[None, :]
    spread = jnp.exp(-jnp.abs(rows - cols) / (1.0 * count))
    noise = jax.random.uniform(keys[0], (count, count), jnp.float32, 0.5, 1.5)
    diagonal = jax.random.uniform(keys[1], (count,), jnp.float32, 0.5, 0.7)
    return (jnp.diag(diagonal) + spread * noise / (1.0 * count)).astype(jnp.float32)


def place_ends(values, own_key, smallest, high):
    shape = values.shape
    place = [jax.random.randint(jax.random.fold_in(own_key, axis), (), 0, shape[axis]) for axis in range(len(shape))]
    values = values.at[tuple(place)].set(smallest)
    longest = shape.index(max(shape))
    place[longest] = (place[longest] + 1) % shape[longest]
    return values.at[tuple(place)].set(high)


def level_of(own_key, dims, cuts, least, high):
    def one(axis_at, blocks):
        heights = jax.random.uniform(jax.random.fold_in(jax.random.fold_in(own_key, 6), axis_at), (blocks,), jnp.float32, least / len(cuts), high / len(cuts))
        return jnp.repeat(jnp.exp(heights), dims[axis_at] // blocks).reshape((-1,) + (1,) * (len(dims) - axis_at - 1))

    loudness = one(*cuts[0])
    for cut in cuts[1:]:
        loudness = loudness * one(*cut)
    return loudness


def normal_values(stream_key, dims, width, bound, cuts=(), kind=jnp.bfloat16):
    values = jax.random.normal(stream_key, dims, jnp.float32) * width
    if len(cuts) > 0:
        values = level_of(stream_key, dims, cuts, -0.22, 0.18) * values
    return jnp.clip(values, min=-bound, max=bound).astype(kind)


def setup_inputs(seed: int = 0) -> dict:
    splits = jax.random.split(jax.random.key(seed), 8)
    return {
        "load": normal_values(splits[0], (NA, NC, 3, R), 1.0, 6.0, ((0, 4), (1, 8)), jnp.float32),
        "region": place_ends(jax.random.randint(splits[1], (NA, NC, R), 0, 2), jax.random.fold_in(splits[1], 1), 0, 1).astype(jnp.int32),
        "family": draw_family(jax.random.fold_in(splits[7], 71), 0),
        "stiffness": jnp.clip(jnp.exp(jax.random.uniform(splits[3], (2, 3), jnp.float32, math.log(1.0), math.log(4.0))), 1.0, 4.0),
        "coupling": jnp.clip(jax.random.uniform(splits[4], (2, 3, 3), jnp.float32, -0.6, 0.6), -0.6, 0.6),
        "line_inverse": draw_line_inverse(jax.random.fold_in(splits[7], 71), 0),
        "axial_inverse": draw_axial_inverse(jax.random.fold_in(splits[7], 71), 0),
    }


PRECISE = lax.Precision.HIGHEST
AXIAL_WEIGHT = 1.0
CIRC_WEIGHT = 1.0
RADIAL_WEIGHT = 1024.0
DAMPING = 0.8


def stencil(padded, stiff_field, fibre_share, coupling, axial_weight):
    centre = padded[1:-1, 1:-1]
    lap_axial = 2.0 * centre - padded[2:, 1:-1] - padded[:-2, 1:-1]
    lap_circ = 2.0 * centre - padded[1:-1, 2:] - padded[1:-1, :-2]
    radial_pad = jnp.pad(centre, ((0, 0), (0, 0), (0, 0), (1, 1)))
    lap_radial = 2.0 * centre - radial_pad[..., 2:] - radial_pad[..., :-2]
    first_mix = jnp.einsum("ce,xyer->xycr", coupling[0], centre, precision=PRECISE)
    second_mix = jnp.einsum("ce,xyer->xycr", coupling[1], centre, precision=PRECISE)
    own_term = centre + first_mix + fibre_share[:, :, None, :] * (second_mix - first_mix)
    return stiff_field * (axial_weight * lap_axial + CIRC_WEIGHT * lap_circ + RADIAL_WEIGHT * lap_radial) + own_term


def line_solve(residual, inverse, axial_matrix):
    radial = jnp.einsum("kij,xykj->xyki", inverse, residual, precision=PRECISE)
    if axial_matrix is None:
        return radial
    return jnp.einsum("ab,bcki->acki", axial_matrix, radial, precision=PRECISE)


def restrict(values):
    return 0.5 * (values[0::2] + values[1::2])


def prolong(values):
    return jnp.repeat(values, 2, axis=0)


def pad_global(field):
    axial = jnp.pad(field, ((1, 1), (0, 0), (0, 0), (0, 0)))
    return jnp.concatenate([axial[:, -1:], axial, axial[:, :1]], axis=1)


def sweeps(solution, rhs, stiff_field, fibre_share, coupling, inverse, axial_weight, number, axial_matrix):
    for turn in range(number):
        if solution is None:
            solution = DAMPING * line_solve(rhs, inverse, axial_matrix)
        else:
            remainder = rhs - stencil(pad_global(solution), stiff_field, fibre_share, coupling, axial_weight)
            solution = solution + DAMPING * line_solve(remainder, inverse, axial_matrix)
    return solution


def reference(load, region, family, stiffness, coupling, line_inverse, axial_inverse):
    stiff0 = jnp.where((region == 0)[:, :, None, :], stiffness[0][None, None, :, None], stiffness[1][None, None, :, None])
    share0 = (family == 1).astype(jnp.float32)
    stiff1, share1 = restrict(stiff0), restrict(share0)
    stiff2, share2 = restrict(stiff1), restrict(share1)
    weights = [AXIAL_WEIGHT, AXIAL_WEIGHT / 4.0, AXIAL_WEIGHT / 16.0]
    fine = sweeps(None, load, stiff0, share0, coupling, line_inverse[0], weights[0], 2, None)
    rhs_mid = restrict(load - stencil(pad_global(fine), stiff0, share0, coupling, weights[0]))
    middle = sweeps(None, rhs_mid, stiff1, share1, coupling, line_inverse[1], weights[1], 2, None)
    rhs_low = restrict(rhs_mid - stencil(pad_global(middle), stiff1, share1, coupling, weights[1]))
    coarse = sweeps(None, rhs_low, stiff2, share2, coupling, line_inverse[2], weights[2], 4, axial_inverse)
    middle = middle + prolong(coarse)
    middle = sweeps(middle, rhs_mid, stiff1, share1, coupling, line_inverse[1], weights[1], 2, None)
    fine = fine + prolong(middle)
    fine = sweeps(fine, load, stiff0, share0, coupling, line_inverse[0], weights[0], 2, None)
    remainder = load - stencil(pad_global(fine), stiff0, share0, coupling, weights[0])
    return fine, remainder, coarse
```

```python
import functools

import jax
import jax.numpy as jnp
from jax import lax
from jax.experimental import pallas as pl
from jax.experimental.pallas import tpu as pltpu
from jax.sharding import PartitionSpec as P

RADIAL_WEIGHT = 1024.0
DAMPING = 0.8
F32 = jnp.float32
BF16 = jnp.bfloat16
DEEP = 4


def kernel(
    dims,
    load_ref,
    region_ref,
    family_ref,
    stiff_ref,
    coup_ref,
    inv_ref,
    axial_ref,
    sol_ref,
    res_ref,
    coarse_ref,
    b0,
    u0a,
    u0b,
    u0c,
    u0d,
    u0e,
    b1,
    u1a,
    u1b,
    u1c,
    u1d,
    u1e,
    b2,
    c2,
    u2,
    y2,
    rbuf,
    reg0,
    sh0,
    reg1,
    sh1,
    ends0,
    ends1,
    wh,
    wm,
    wl,
    wtmp,
    pack0,
    got0,
    pack1,
    got1,
    packc,
    gotc,
    packb,
    gotb,
    send_sem,
    recv_sem,
    gsend,
    grecv,
    csend,
    crecv,
):
    nax, ncirc, ca, cc, rr, lanes = dims
    ce = cc + 2 * DEEP
    cm, cq = ca // 2, ca // 4
    na2 = cq * nax
    pos = lax.axis_index("ax")
    me_c = lax.axis_index("circ")
    ax_left, ax_right = lax.rem(pos + nax - 1, nax), lax.rem(pos + 1, nax)
    c_left, c_right = lax.rem(me_c + ncirc - 1, ncirc), lax.rem(me_c + 1, ncirc)
    has_left, has_right = pos > 0, pos < nax - 1

    barrier = pltpu.get_barrier_semaphore()
    for d in range(1, nax):
        pl.semaphore_signal(barrier, inc=1, device_id=(lax.rem(pos + d, nax), me_c))
    pl.semaphore_signal(barrier, inc=1, device_id=(pos, c_left))
    pl.semaphore_signal(barrier, inc=1, device_id=(pos, c_right))

    b0[:, 1 : ca + 1, 0:cc, lanes - 128 : lanes] = jnp.zeros((3, ca, cc, 128), F32)
    for k in range(3):
        b0[k, 1 : ca + 1, 0:cc, 0:rr] = load_ref[:, k]

    def zero_row(buf, row):
        buf[:, row] = jnp.zeros((3, ce, lanes), F32)

    @pl.when(jnp.logical_not(has_left))
    def _():
        for buf in (b0, u0b, u1a, u1b, u1d, u1e, u0d, u0e):
            zero_row(buf, 0)

    @pl.when(jnp.logical_not(has_right))
    def _():
        for buf, row in (
            (b0, ca + 1),
            (u0b, ca + 1),
            (u0d, ca + 1),
            (u0e, ca + 1),
            (u1a, cm + 1),
            (u1b, cm + 1),
            (u1d, cm + 1),
            (u1e, cm + 1),
        ):
            zero_row(buf, row)

    zero_row(u2, 0)
    zero_row(u2, na2 + 1)

    def edge_copies(x, buf, rows, pack, got):
        left = pltpu.make_async_remote_copy(
            src_ref=buf.at[:, 1, 0:cc],
            dst_ref=buf.at[:, rows + 1, 0:cc],
            send_sem=send_sem.at[x, 0],
            recv_sem=recv_sem.at[x, 1],
            device_id=(ax_left, me_c),
        )
        right = pltpu.make_async_remote_copy(
            src_ref=buf.at[:, rows, 0:cc],
            dst_ref=buf.at[:, 0, 0:cc],
            send_sem=send_sem.at[x, 1],
            recv_sem=recv_sem.at[x, 0],
            device_id=(ax_right, me_c),
        )
        down = pltpu.make_async_remote_copy(
            src_ref=pack.at[0],
            dst_ref=got.at[0],
            send_sem=send_sem.at[x, 2],
            recv_sem=recv_sem.at[x, 2],
            device_id=(pos, c_left),
        )
        up = pltpu.make_async_remote_copy(
            src_ref=pack.at[1],
            dst_ref=got.at[1],
            send_sem=send_sem.at[x, 3],
            recv_sem=recv_sem.at[x, 3],
            device_id=(pos, c_right),
        )
        return left, right, down, up

    def edge_start(x, buf, rows, pack, got):
        left, right, down, up = edge_copies(x, buf, rows, pack, got)
        for k in range(3):
            for a in range(rows):
                pack[0, k * rows + a : k * rows + a + 1, :] = buf[k, a + 1, 0:1, :]
                pack[1, k * rows + a : k * rows + a + 1, :] = buf[k, a + 1, cc - 1 : cc, :]
        down.start()
        up.start()

        @pl.when(has_left)
        def _():
            left.start()

        @pl.when(has_right)
        def _():
            right.start()

    def edge_finish(x, buf, rows, pack, got, keep=False):
        left, right, down, up = edge_copies(x, buf, rows, pack, got)
        down.wait()
        up.wait()
        for k in range(3 if keep else 0):
            for a in range(rows):
                buf[k, a + 1, cc : cc + 1, :] = got[0, k * rows + a : k * rows + a + 1, :]
                buf[k, a + 1, ce - 1 : ce, :] = got[1, k * rows + a : k * rows + a + 1, :]

        @pl.when(has_left)
        def _():
            left.wait_send()
            right.wait_recv()

        @pl.when(has_right)
        def _():
            right.wait_send()
            left.wait_recv()

    def gather_copies(which, buf):
        pairs = []
        for d in range(1, nax):
            to, of = lax.rem(pos + d, nax), lax.rem(pos + nax - d, nax)
            out = pltpu.make_async_remote_copy(
                src_ref=buf.at[:, pl.ds(pos * cq, cq), 0:cc],
                dst_ref=buf.at[:, pl.ds(pos * cq, cq), 0:cc],
                send_sem=gsend.at[which, d],
                recv_sem=grecv.at[which, d],
                device_id=(to, me_c),
            )
            come = pltpu.make_async_remote_copy(
                src_ref=buf.at[:, pl.ds(of * cq, cq), 0:cc],
                dst_ref=buf.at[:, pl.ds(of * cq, cq), 0:cc],
                send_sem=gsend.at[which, d],
                recv_sem=grecv.at[which, d],
                device_id=(to, me_c),
            )
            pairs.append((out, come))
        return pairs

    half = na2 // 2
    low = lax.broadcasted_iota(jnp.int32, (8, lanes), 0) < DEEP

    def turn(tile):
        return pltpu.roll(tile, DEEP, 0)

    def deep_copies(which, pack, got):
        return [
            pltpu.make_async_remote_copy(
                src_ref=pack.at[side],
                dst_ref=got.at[side],
                send_sem=csend.at[which, side],
                recv_sem=crecv.at[which, side],
                device_id=(pos, (c_left, c_right)[side]),
            )
            for side in range(2)
        ]

    def deep_start(which, buf, fields, pack, got):
        for f in range(fields):
            for a in range(half):
                pack[0, f, a] = jnp.where(low, buf[f, a, 0:8, :], turn(buf[f, a + half, 0:8, :]))
                pack[1, f, a] = jnp.where(
                    low, turn(buf[f, a, cc - 8 : cc, :]), buf[f, a + half, cc - 8 : cc, :]
                )
        for copy in deep_copies(which, pack, got):
            copy.start()

    def deep_finish(which, buf, fields, pack, got):
        for copy in deep_copies(which, pack, got):
            copy.wait()
        for f in range(fields):
            for a in range(half):
                right, left = got[0, f, a], got[1, f, a]
                buf[f, a, cc:ce, :] = jnp.where(low, right, turn(left))
                buf[f, a + half, cc:ce, :] = jnp.where(low, turn(right), left)

    def split(x):
        hi = x.astype(BF16)
        rest = x - hi.astype(F32)
        mid = rest.astype(BF16)
        return hi, mid, (rest - mid.astype(F32)).astype(BF16)

    def line(level, k, x):
        hi, mid, lo = split(x)
        i = level * 3 + k
        dot = functools.partial(jnp.dot, preferred_element_type=F32)
        small = dot(lo, wh[i]) + dot(hi, wl[i]) + dot(mid, wm[i])
        return dot(hi, wh[i]) + (dot(mid, wh[i]) + dot(hi, wm[i]) + small)

    stiff = [[stiff_ref[s, k] for k in range(3)] for s in range(2)]
    first = [[coup_ref[k, 0, e] for e in range(3)] for k in range(3)]
    diff = [[coup_ref[k, 1, e] - first[k][e] for e in range(3)] for k in range(3)]

    coefs = [(reg0, sh0), (reg1, sh1), (c2.at[0], c2.at[1])]
    edges = [ends0, ends1]

    def remainder(u, level, begin, count, stride, cols, rhs, shift, wrap):
        weight, (reg, share) = 0.25**level, coefs[level]
        gain = [stiff[1][k] - stiff[0][k] for k in range(3)]

        def row(step, carry):
            a = begin + step * stride
            own = [u[k, a + 1, 0:cols, :] for k in range(3)]
            region, fibre = reg[a, 0:cols, :], share[a, 0:cols, :]
            for k in range(3):
                c = own[k]
                if wrap:
                    around = pltpu.roll(c, 1, 0) + pltpu.roll(c, cols - 1, 0)
                else:
                    wide = u[k, a + 1]
                    around = pltpu.roll(wide, 1, 0)[0:cols] + pltpu.roll(wide, ce - 1, 0)[0:cols]
                beside = pltpu.roll(c, 1, 1) + pltpu.roll(c, lanes - 1, 1)
                axial = u[k, a, 0:cols, :] + u[k, a + 2, 0:cols, :]
                lap = (
                    (2.0 * weight + 2.0 + 2.0 * RADIAL_WEIGHT) * c
                    - weight * axial
                    - around
                    - RADIAL_WEIGHT * beside
                )
                mix = own[0] * first[k][0] + own[1] * first[k][1] + own[2] * first[k][2]
                more = own[0] * diff[k][0] + own[1] * diff[k][1] + own[2] * diff[k][2]
                value = (stiff[0][k] + region * gain[k]) * lap + (c + mix + fibre * more)
                rbuf[k, pl.ds(pl.multiple_of(a * cols, 8), cols), :] = (
                    rhs[k, a + shift, 0:cols, :] - value
                )
            return carry

        lax.fori_loop(0, count, row, 0)

    def whole_remainder(u, level, rows, rhs):
        remainder(u, level, 0, rows, 1, cc, rhs, 1, False)

    def edge_remainder(x, u, level, rows, rhs, pack, got, keep=False, between=None):
        edge_start(x, u, rows, pack, got)
        remainder(u, level, 1, rows - 2, 1, cc, rhs, 1, True)
        if between is not None:
            between()
        edge_finish(x, u, rows, pack, got, keep)
        remainder(u, level, 0, 2, rows - 1, cc, rhs, 1, True)
        ends = edges[level]
        for k in range(3):
            at = k * rows
            for side, col in ((0, cc - 1), (1, 0)):
                coef = stiff[0][k] + ends[side, 0:rows, :] * (stiff[1][k] - stiff[0][k])
                more = coef * (got[side, at : at + rows, :] - pack[side, at : at + rows, :])
                for a in range(rows):
                    place = a * cc + col
                    rbuf[k, place : place + 1, :] = rbuf[k, place : place + 1, :] + more[a : a + 1]

    def correct(level, rows, old, new):
        def one(k, carry):
            step = line(level, k, rbuf[k, 0 : rows * cc, :]).reshape(rows, cc, lanes)
            new[k, 1 : rows + 1, 0:cc, :] = old[k, 1 : rows + 1, 0:cc, :] + step
            return carry

        lax.fori_loop(0, 3, one, 0)

    def first_sweep(level, rhs, rows, new):
        def one(k, carry):
            step = line(level, k, rhs[k].reshape(rows * ce, lanes))
            new[k] = step.reshape(rows, ce, lanes)
            return carry

        lax.fori_loop(0, 3, one, 0)

    def start_from(level, rhs, rows, new):
        def one(k, carry):
            step = line(level, k, rhs[k, 1 : rows + 1, 0:cc, :].reshape(rows * cc, lanes))
            new[k, 1 : rows + 1, 0:cc, :] = step.reshape(rows, cc, lanes)
            return carry

        lax.fori_loop(0, 3, one, 0)

    def restrict_into(rows, write):
        for k in range(3):
            r = rbuf[k, 0 : rows * cc, :].reshape(rows // 2, 2, cc, lanes)
            write(k, 0.5 * (r[:, 0] + r[:, 1]))

    pl.semaphore_wait(barrier, nax + 1)
    edge_start(0, b0, ca, pack0, got0)

    zeros = jnp.zeros((ca, cc, lanes), F32)
    reg0[...] = zeros
    sh0[...] = zeros
    reg0[:, :, 0:rr] = jnp.where(region_ref[...] == 0, 0.0, 1.0)
    sh0[:, :, 0:rr] = jnp.where(family_ref[...] == 1, 1.0, 0.0)
    for fine_c, mid_c, f in ((reg0, reg1, 0), (sh0, sh1, 1)):
        for a in range(cm):
            mid_c[a] = 0.5 * (fine_c[2 * a] + fine_c[2 * a + 1])
        for a in range(cq):
            c2[f, pos * cq + a, 0:cc, :] = 0.5 * (mid_c[2 * a] + mid_c[2 * a + 1])
    for out, _ in gather_copies(0, c2):
        out.start()
    for ends, reg, rows in ((ends0, reg0, ca), (ends1, reg1, cm)):
        for a in range(rows):
            ends[0, a : a + 1, :] = reg[a, cc - 1 : cc, :]
            ends[1, a : a + 1, :] = reg[a, 0:1, :]

    wtmp[...] = jnp.zeros((lanes, lanes), F32)

    def prepare(i, carry):
        wtmp[0:rr, 0:rr] = inv_ref[i] * DAMPING
        wh[i], wm[i], wl[i] = split(jnp.transpose(wtmp[...]))
        return carry

    lax.fori_loop(0, 9, prepare, 0)

    edge_finish(0, b0, ca, pack0, got0, True)
    first_sweep(0, b0, ca + 2, u0a)
    whole_remainder(u0a, 0, ca, b0)
    correct(0, ca, u0a, u0b)

    def coefficients_on():
        for out, come in gather_copies(0, c2):
            out.wait_send()
            come.wait_recv()
        deep_start(0, c2, 2, packc, gotc)

    edge_remainder(1, u0b, 0, ca, b0, pack0.at[2:4], got0.at[2:4], True, coefficients_on)

    def into_b1(k, value):
        b1[k, 1 : cm + 1, 0:cc, :] = value

    restrict_into(ca, into_b1)

    start_from(1, b1, cm, u1a)
    edge_remainder(2, u1a, 1, cm, b1, pack1, got1)
    correct(1, cm, u1a, u1b)
    edge_remainder(3, u1b, 1, cm, b1, pack1.at[2:4], got1.at[2:4], True)

    def into_b2(k, value):
        b2[k, pl.ds(pos * cq, cq), 0:cc, :] = value

    restrict_into(cm, into_b2)

    for out, _ in gather_copies(1, b2):
        out.start()
    deep_finish(0, c2, 2, packc, gotc)
    for out, come in gather_copies(1, b2):
        out.wait_send()
        come.wait_recv()
    deep_start(1, b2, 3, packb, gotb)
    deep_finish(1, b2, 3, packb, gotb)

    def coarse_solve(first_time):
        def one(k, carry):
            x = b2[k].reshape(na2 * ce, lanes) if first_time else rbuf[k, 0 : na2 * ce, :]
            y2[...] = line(2, k, x).reshape(na2, ce, lanes)

            def row(a, inner):
                total = axial_ref[a, 0] * y2[0]
                for b in range(1, na2):
                    total = total + axial_ref[a, b] * y2[b]
                u2[k, a + 1] = total if first_time else u2[k, a + 1] + total
                return inner

            return lax.fori_loop(0, na2, row, carry)

        lax.fori_loop(0, 3, one, 0)

    coarse_solve(True)

    def coarse_sweep(turn_number, carry):
        remainder(u2, 2, 0, na2, 1, ce, b2, 0, True)
        coarse_solve(False)
        return carry

    lax.fori_loop(0, 3, coarse_sweep, 0)

    for a in range(cq):
        for k in range(3):
            coarse_ref[a, k] = u2[k, pos * cq + a + 1, 0:cc, 0:rr]

    for i in range(cm + 2):
        for k in range(3):
            u1c[k, i] = u1b[k, i] + u2[k, pos * cq + (i + 1) // 2]
    whole_remainder(u1c, 1, cm, b1)
    correct(1, cm, u1c, u1d)
    edge_remainder(4, u1d, 1, cm, b1, pack1.at[4:6], got1.at[4:6])
    correct(1, cm, u1d, u1e)
    edge_start(5, u1e, cm, pack1.at[6:8], got1.at[6:8])
    edge_finish(5, u1e, cm, pack1.at[6:8], got1.at[6:8], True)

    for i in range(ca + 2):
        for k in range(3):
            u0c[k, i] = u0b[k, i] + u1e[k, (i + 1) // 2]
    whole_remainder(u0c, 0, ca, b0)
    correct(0, ca, u0c, u0d)
    edge_remainder(6, u0d, 0, ca, b0, pack0.at[4:6], got0.at[4:6])
    correct(0, ca, u0d, u0e)

    def solution_out():
        for k in range(3):
            sol_ref[:, k] = u0e[k, 1 : ca + 1, 0:cc, 0:rr]

    edge_remainder(7, u0e, 0, ca, b0, pack0.at[6:8], got0.at[6:8], False, solution_out)
    for k in range(3):
        res_ref[:, k] = rbuf[k, 0 : ca * cc, 0:rr].reshape(ca, cc, rr)


def body(load, region, family, stiffness, coupling, line_inverse, axial_inverse):
    nax, ncirc = lax.axis_size("ax"), lax.axis_size("circ")
    ca, cc, _, rr = load.shape
    lanes = -(-rr // 128) * 128
    ce = cc + 2 * DEEP
    cm, cq = ca // 2, ca // 4
    na2 = cq * nax
    rows = max(ca * cc, na2 * ce)
    rows1 = -(-3 * cm // 8) * 8
    vmem = pl.BlockSpec(memory_space=pltpu.VMEM)
    smem = pl.BlockSpec(memory_space=pltpu.SMEM)
    fine = pltpu.VMEM((3, ca + 2, ce, lanes), F32)
    mid = pltpu.VMEM((3, cm + 2, ce, lanes), F32)
    half = na2 // 2
    sol, res, coarse = pl.pallas_call(
        functools.partial(kernel, (nax, ncirc, ca, cc, rr, lanes)),
        out_shape=[
            jax.ShapeDtypeStruct((ca, 3, cc, rr), F32),
            jax.ShapeDtypeStruct((ca, 3, cc, rr), F32),
            jax.ShapeDtypeStruct((cq, 3, cc, rr), F32),
        ],
        in_specs=[vmem, vmem, vmem, smem, smem, vmem, smem],
        out_specs=[vmem, vmem, vmem],
        scratch_shapes=[fine] * 6
        + [mid] * 6
        + [
            pltpu.VMEM((3, na2, ce, lanes), F32),
            pltpu.VMEM((2, na2, ce, lanes), F32),
            pltpu.VMEM((3, na2 + 2, ce, lanes), F32),
            pltpu.VMEM((na2, ce, lanes), F32),
            pltpu.VMEM((3, rows, lanes), F32),
            pltpu.VMEM((ca, cc, lanes), F32),
            pltpu.VMEM((ca, cc, lanes), F32),
            pltpu.VMEM((cm, cc, lanes), F32),
            pltpu.VMEM((cm, cc, lanes), F32),
            pltpu.VMEM((2, ca, lanes), F32),
            pltpu.VMEM((2, cm, lanes), F32),
            pltpu.VMEM((9, lanes, lanes), BF16),
            pltpu.VMEM((9, lanes, lanes), BF16),
            pltpu.VMEM((9, lanes, lanes), BF16),
            pltpu.VMEM((lanes, lanes), F32),
            pltpu.VMEM((8, 3 * ca, lanes), F32),
            pltpu.VMEM((8, 3 * ca, lanes), F32),
            pltpu.VMEM((8, rows1, lanes), F32),
            pltpu.VMEM((8, rows1, lanes), F32),
            pltpu.VMEM((2, 2, half, 8, lanes), F32),
            pltpu.VMEM((2, 2, half, 8, lanes), F32),
            pltpu.VMEM((2, 3, half, 8, lanes), F32),
            pltpu.VMEM((2, 3, half, 8, lanes), F32),
            pltpu.SemaphoreType.DMA((8, 4)),
            pltpu.SemaphoreType.DMA((8, 4)),
            pltpu.SemaphoreType.DMA((2, nax)),
            pltpu.SemaphoreType.DMA((2, nax)),
            pltpu.SemaphoreType.DMA((2, 2)),
            pltpu.SemaphoreType.DMA((2, 2)),
        ],
        compiler_params=pltpu.CompilerParams(
            collective_id=0, has_side_effects=True, vmem_limit_bytes=52 * 1024 * 1024
        ),
        name="vcycle",
    )(
        jnp.transpose(load, (0, 2, 1, 3)),
        region,
        family,
        stiffness,
        jnp.transpose(coupling, (1, 0, 2)),
        line_inverse.reshape(9, rr, rr),
        axial_inverse,
    )
    back = (0, 2, 1, 3)
    return jnp.transpose(sol, back), jnp.transpose(res, back), jnp.transpose(coarse, back)


def solution(mesh):
    field, cells = P("ax", "circ", None, None), P("ax", "circ", None)
    return jax.shard_map(
        body,
        mesh=mesh,
        in_specs=(field, cells, cells, P(), P(), P(), P()),
        out_specs=(field, field, field),
        check_vma=False,
    )
```

```python
import functools

import jax
import jax.numpy as jnp
from jax import lax
from jax.experimental import pallas as pl
from jax.experimental.pallas import tpu as pltpu
from jax.sharding import PartitionSpec as P

RADIAL_WEIGHT = 1024.0
DAMPING = 0.8
F32 = jnp.float32
BF16 = jnp.bfloat16
DEEP = 4


def kernel(
    dims,
    load_hbm,
    region_hbm,
    family_hbm,
    stiff_hbm,
    coup_hbm,
    inv_hbm,
    axial_hbm,
    sol_ref,
    res_ref,
    coarse_ref,
    load_ref,
    region_ref,
    family_ref,
    stiff_ref,
    coup_ref,
    inv_ref,
    axial_ref,
    in_sem,
    b0,
    u0a,
    u0b,
    u0c,
    u0d,
    u0e,
    b1,
    u1a,
    u1b,
    u1c,
    u1d,
    u1e,
    b2,
    c2,
    u2,
    y2,
    rbuf,
    reg0,
    sh0,
    reg1,
    sh1,
    ends0,
    ends1,
    wh,
    wm,
    wl,
    wtmp,
    pack0,
    got0,
    pack1,
    got1,
    packc,
    gotc,
    packb,
    gotb,
    send_sem,
    recv_sem,
    gsend,
    grecv,
    csend,
    crecv,
):
    nax, ncirc, ca, cc, rr, lanes = dims
    ce = cc + 2 * DEEP
    cm, cq = ca // 2, ca // 4
    na2 = cq * nax
    pos = lax.axis_index("ax")
    me_c = lax.axis_index("circ")
    ax_left, ax_right = lax.rem(pos + nax - 1, nax), lax.rem(pos + 1, nax)
    c_left, c_right = lax.rem(me_c + ncirc - 1, ncirc), lax.rem(me_c + 1, ncirc)
    has_left, has_right = pos > 0, pos < nax - 1

    arrivals = [
        pltpu.make_async_copy(source, target, in_sem.at[i])
        for i, (source, target) in enumerate(
            (
                (load_hbm, load_ref),
                (region_hbm, region_ref),
                (family_hbm, family_ref),
                (stiff_hbm, stiff_ref),
                (coup_hbm, coup_ref),
                (inv_hbm, inv_ref),
                (axial_hbm, axial_ref),
            )
        )
    ]
    for arrival in arrivals:
        arrival.start()

    barrier = pltpu.get_barrier_semaphore()
    for d in range(1, nax):
        pl.semaphore_signal(barrier, inc=1, device_id=(lax.rem(pos + d, nax), me_c))
    pl.semaphore_signal(barrier, inc=1, device_id=(pos, c_left))
    pl.semaphore_signal(barrier, inc=1, device_id=(pos, c_right))

    b0[:, 1 : ca + 1, 0:cc, lanes - 128 : lanes] = jnp.zeros((3, ca, cc, 128), F32)
    arrivals[0].wait()
    for k in range(3):
        b0[k, 1 : ca + 1, 0:cc, 0:rr] = load_ref[:, k]

    def zero_row(buf, row):
        buf[:, row] = jnp.zeros((3, ce, lanes), F32)

    @pl.when(jnp.logical_not(has_left))
    def _():
        for buf in (b0, u0b, u1a, u1b, u1d, u1e, u0d, u0e):
            zero_row(buf, 0)

    @pl.when(jnp.logical_not(has_right))
    def _():
        for buf, row in (
            (b0, ca + 1),
            (u0b, ca + 1),
            (u0d, ca + 1),
            (u0e, ca + 1),
            (u1a, cm + 1),
            (u1b, cm + 1),
            (u1d, cm + 1),
            (u1e, cm + 1),
        ):
            zero_row(buf, row)

    zero_row(u2, 0)
    zero_row(u2, na2 + 1)

    def edge_copies(x, buf, rows, pack, got):
        left = pltpu.make_async_remote_copy(
            src_ref=buf.at[:, 1, 0:cc],
            dst_ref=buf.at[:, rows + 1, 0:cc],
            send_sem=send_sem.at[x, 0],
            recv_sem=recv_sem.at[x, 1],
            device_id=(ax_left, me_c),
        )
        right = pltpu.make_async_remote_copy(
            src_ref=buf.at[:, rows, 0:cc],
            dst_ref=buf.at[:, 0, 0:cc],
            send_sem=send_sem.at[x, 1],
            recv_sem=recv_sem.at[x, 0],
            device_id=(ax_right, me_c),
        )
        down = pltpu.make_async_remote_copy(
            src_ref=pack.at[0],
            dst_ref=got.at[0],
            send_sem=send_sem.at[x, 2],
            recv_sem=recv_sem.at[x, 2],
            device_id=(pos, c_left),
        )
        up = pltpu.make_async_remote_copy(
            src_ref=pack.at[1],
            dst_ref=got.at[1],
            send_sem=send_sem.at[x, 3],
            recv_sem=recv_sem.at[x, 3],
            device_id=(pos, c_right),
        )
        return left, right, down, up

    def edge_start(x, buf, rows, pack, got):
        left, right, down, up = edge_copies(x, buf, rows, pack, got)
        for k in range(3):
            for a in range(rows):
                pack[0, k * rows + a : k * rows + a + 1, :] = buf[k, a + 1, 0:1, :]
                pack[1, k * rows + a : k * rows + a + 1, :] = buf[k, a + 1, cc - 1 : cc, :]
        down.start()
        up.start()

        @pl.when(has_left)
        def _():
            left.start()

        @pl.when(has_right)
        def _():
            right.start()

    def edge_finish(x, buf, rows, pack, got, keep=False):
        left, right, down, up = edge_copies(x, buf, rows, pack, got)
        down.wait()
        up.wait()
        for k in range(3 if keep else 0):
            for a in range(rows):
                buf[k, a + 1, cc : cc + 1, :] = got[0, k * rows + a : k * rows + a + 1, :]
                buf[k, a + 1, ce - 1 : ce, :] = got[1, k * rows + a : k * rows + a + 1, :]

        @pl.when(has_left)
        def _():
            left.wait_send()
            right.wait_recv()

        @pl.when(has_right)
        def _():
            right.wait_send()
            left.wait_recv()

    mate = pos + 1 - 2 * lax.rem(pos, 2)

    def block_copy(which, slot, buf, cols, block, to):
        part = (slice(None), pl.ds(block * cq, cq), slice(*cols))
        return pltpu.make_async_remote_copy(
            src_ref=buf.at[part],
            dst_ref=buf.at[part],
            send_sem=gsend.at[which, slot],
            recv_sem=grecv.at[which, slot],
            device_id=(to, me_c),
        )

    def across(j):
        return lax.rem(pos + 2 * j, nax), lax.rem(pos + nax - 2 * j, nax)

    def gather_start(which, buf, cols):
        for j in range(1, nax // 2):
            block_copy(which, j, buf, cols, pos, across(j)[0]).start()
        block_copy(which, 0, buf, cols, pos, mate).start()

    def gather_forward(which, buf, cols):
        for j in range(1, nax // 2):
            block_copy(which, j, buf, cols, across(j)[1], across(j)[0]).wait_recv()
            block_copy(which, nax // 2 + j, buf, cols, across(j)[1], mate).start()

    def gather_finish(which, buf, cols):
        for j in range(1, nax // 2):
            block_copy(which, j, buf, cols, pos, across(j)[0]).wait_send()
            block_copy(which, nax // 2 + j, buf, cols, across(j)[1], mate).wait_send()
            theirs = lax.rem(mate + nax - 2 * j, nax)
            block_copy(which, nax // 2 + j, buf, cols, theirs, mate).wait_recv()
        block_copy(which, 0, buf, cols, pos, mate).wait_send()
        block_copy(which, 0, buf, cols, mate, mate).wait_recv()

    half = cq // 2
    base = pos * cq
    low = lax.broadcasted_iota(jnp.int32, (8, lanes), 0) < DEEP

    def turn(tile):
        return pltpu.roll(tile, DEEP, 0)

    def deep_copies(which, pack, got):
        return [
            pltpu.make_async_remote_copy(
                src_ref=pack.at[side],
                dst_ref=got.at[side],
                send_sem=csend.at[which, side],
                recv_sem=crecv.at[which, side],
                device_id=(pos, (c_left, c_right)[side]),
            )
            for side in range(2)
        ]

    def deep_start(which, buf, fields, pack, got):
        for f in range(fields):
            for a in range(half):
                pack[0, f, a] = jnp.where(low, buf[f, base + a, 0:8, :], turn(buf[f, base + a + half, 0:8, :]))
                pack[1, f, a] = jnp.where(
                    low,
                    turn(buf[f, base + a, cc - 8 : cc, :]),
                    buf[f, base + a + half, cc - 8 : cc, :],
                )
        for copy in deep_copies(which, pack, got):
            copy.start()

    def deep_finish(which, buf, fields, pack, got):
        for copy in deep_copies(which, pack, got):
            copy.wait()
        for f in range(fields):
            for a in range(half):
                right, left = got[0, f, a], got[1, f, a]
                buf[f, base + a, cc:ce, :] = jnp.where(low, right, turn(left))
                buf[f, base + a + half, cc:ce, :] = jnp.where(low, turn(right), left)

    def split(x):
        hi = x.astype(BF16)
        rest = x - hi.astype(F32)
        mid = rest.astype(BF16)
        return hi, mid, (rest - mid.astype(F32)).astype(BF16)

    def line(level, k, x):
        hi, mid, lo = split(x)
        i = level * 3 + k
        dot = functools.partial(jnp.dot, preferred_element_type=F32)
        small = dot(lo, wh[i]) + dot(hi, wl[i]) + dot(mid, wm[i])
        return dot(hi, wh[i]) + (dot(mid, wh[i]) + dot(hi, wm[i]) + small)

    arrivals[3].wait()
    arrivals[4].wait()
    stiff = [[stiff_ref[s, k] for k in range(3)] for s in range(2)]
    first = [[coup_ref[k, 0, e] for e in range(3)] for k in range(3)]
    diff = [[coup_ref[k, 1, e] - first[k][e] for e in range(3)] for k in range(3)]

    coefs = [(reg0, sh0), (reg1, sh1), (c2.at[0], c2.at[1])]
    edges = [ends0, ends1]

    def remainder(u, level, begin, count, stride, cols, rhs, shift, wrap):
        weight, (reg, share) = 0.25**level, coefs[level]
        gain = [stiff[1][k] - stiff[0][k] for k in range(3)]

        def row(step, carry):
            a = begin + step * stride
            own = [u[k, a + 1, 0:cols, :] for k in range(3)]
            region, fibre = reg[a, 0:cols, :], share[a, 0:cols, :]
            for k in range(3):
                c = own[k]
                if wrap:
                    around = pltpu.roll(c, 1, 0) + pltpu.roll(c, cols - 1, 0)
                else:
                    wide = u[k, a + 1]
                    around = pltpu.roll(wide, 1, 0)[0:cols] + pltpu.roll(wide, ce - 1, 0)[0:cols]
                beside = pltpu.roll(c, 1, 1) + pltpu.roll(c, lanes - 1, 1)
                axial = u[k, a, 0:cols, :] + u[k, a + 2, 0:cols, :]
                lap = (
                    (2.0 * weight + 2.0 + 2.0 * RADIAL_WEIGHT) * c
                    - weight * axial
                    - around
                    - RADIAL_WEIGHT * beside
                )
                mix = own[0] * first[k][0] + own[1] * first[k][1] + own[2] * first[k][2]
                more = own[0] * diff[k][0] + own[1] * diff[k][1] + own[2] * diff[k][2]
                value = (stiff[0][k] + region * gain[k]) * lap + (c + mix + fibre * more)
                rbuf[k, pl.ds(pl.multiple_of(a * cols, 8), cols), :] = (
                    rhs[k, a + shift, 0:cols, :] - value
                )
            return carry

        lax.fori_loop(0, count, row, 0)

    def whole_remainder(u, level, rows, rhs):
        remainder(u, level, 0, rows, 1, cc, rhs, 1, False)

    def edge_remainder(x, u, level, rows, rhs, pack, got, keep=False, between=None):
        edge_start(x, u, rows, pack, got)
        remainder(u, level, 1, rows - 2, 1, cc, rhs, 1, True)
        if between is not None:
            between()
        edge_finish(x, u, rows, pack, got, keep)
        remainder(u, level, 0, 2, rows - 1, cc, rhs, 1, True)
        ends = edges[level]
        for k in range(3):
            at = k * rows
            for side, col in ((0, cc - 1), (1, 0)):
                coef = stiff[0][k] + ends[side, 0:rows, :] * (stiff[1][k] - stiff[0][k])
                more = coef * (got[side, at : at + rows, :] - pack[side, at : at + rows, :])
                for a in range(rows):
                    place = a * cc + col
                    rbuf[k, place : place + 1, :] = rbuf[k, place : place + 1, :] + more[a : a + 1]

    def correct(level, rows, old, new):
        def one(k, carry):
            step = line(level, k, rbuf[k, 0 : rows * cc, :]).reshape(rows, cc, lanes)
            new[k, 1 : rows + 1, 0:cc, :] = old[k, 1 : rows + 1, 0:cc, :] + step
            return carry

        lax.fori_loop(0, 3, one, 0)

    def first_sweep(level, rhs, rows, new):
        def one(k, carry):
            step = line(level, k, rhs[k].reshape(rows * ce, lanes))
            new[k] = step.reshape(rows, ce, lanes)
            return carry

        lax.fori_loop(0, 3, one, 0)

    def start_from(level, rhs, rows, new):
        def one(k, carry):
            step = line(level, k, rhs[k, 1 : rows + 1, 0:cc, :].reshape(rows * cc, lanes))
            new[k, 1 : rows + 1, 0:cc, :] = step.reshape(rows, cc, lanes)
            return carry

        lax.fori_loop(0, 3, one, 0)

    def restrict_into(rows, write):
        for k in range(3):
            r = rbuf[k, 0 : rows * cc, :].reshape(rows // 2, 2, cc, lanes)
            write(k, 0.5 * (r[:, 0] + r[:, 1]))

    pl.semaphore_wait(barrier, nax + 1)
    edge_start(0, b0, ca, pack0, got0)

    zeros = jnp.zeros((ca, cc, lanes), F32)
    arrivals[1].wait()
    arrivals[2].wait()
    reg0[...] = zeros
    sh0[...] = zeros
    reg0[:, :, 0:rr] = jnp.where(region_ref[...] == 0, 0.0, 1.0)
    sh0[:, :, 0:rr] = jnp.where(family_ref[...] == 1, 1.0, 0.0)
    for fine_c, mid_c, f in ((reg0, reg1, 0), (sh0, sh1, 1)):
        for a in range(cm):
            mid_c[a] = 0.5 * (fine_c[2 * a] + fine_c[2 * a + 1])
        for a in range(cq):
            c2[f, pos * cq + a, 0:cc, :] = 0.5 * (mid_c[2 * a] + mid_c[2 * a + 1])
    gather_start(0, c2, (0, cc))
    deep_start(0, c2, 2, packc, gotc)
    for ends, reg, rows in ((ends0, reg0, ca), (ends1, reg1, cm)):
        for a in range(rows):
            ends[0, a : a + 1, :] = reg[a, cc - 1 : cc, :]
            ends[1, a : a + 1, :] = reg[a, 0:1, :]

    arrivals[5].wait()
    arrivals[6].wait()
    wtmp[...] = jnp.zeros((lanes, lanes), F32)

    def prepare(i, carry):
        wtmp[0:rr, 0:rr] = inv_ref[i] * DAMPING
        wh[i], wm[i], wl[i] = split(jnp.transpose(wtmp[...]))
        return carry

    lax.fori_loop(0, 9, prepare, 0)

    edge_finish(0, b0, ca, pack0, got0, True)
    first_sweep(0, b0, ca + 2, u0a)
    whole_remainder(u0a, 0, ca, b0)
    correct(0, ca, u0a, u0b)

    def coefficients_on():
        deep_finish(0, c2, 2, packc, gotc)
        gather_start(1, c2, (cc, ce))
        gather_forward(0, c2, (0, cc))
        gather_finish(0, c2, (0, cc))

    edge_remainder(1, u0b, 0, ca, b0, pack0.at[2:4], got0.at[2:4], True, coefficients_on)

    def into_b1(k, value):
        b1[k, 1 : cm + 1, 0:cc, :] = value

    restrict_into(ca, into_b1)

    start_from(1, b1, cm, u1a)
    edge_remainder(2, u1a, 1, cm, b1, pack1, got1)
    correct(1, cm, u1a, u1b)
    edge_remainder(3, u1b, 1, cm, b1, pack1.at[2:4], got1.at[2:4], True)

    def into_b2(k, value):
        b2[k, pl.ds(pos * cq, cq), 0:cc, :] = value

    restrict_into(cm, into_b2)

    deep_start(1, b2, 3, packb, gotb)
    gather_start(2, b2, (0, cc))
    gather_forward(1, c2, (cc, ce))
    gather_finish(1, c2, (cc, ce))
    gather_forward(2, b2, (0, cc))
    deep_finish(1, b2, 3, packb, gotb)
    gather_start(3, b2, (cc, ce))
    gather_forward(3, b2, (cc, ce))
    gather_finish(2, b2, (0, cc))
    gather_finish(3, b2, (cc, ce))

    def coarse_solve(first_time):
        def one(k, carry):
            x = b2[k].reshape(na2 * ce, lanes) if first_time else rbuf[k, 0 : na2 * ce, :]
            y2[...] = line(2, k, x).reshape(na2, ce, lanes)

            def row(a, inner):
                total = axial_ref[a, 0] * y2[0]
                for b in range(1, na2):
                    total = total + axial_ref[a, b] * y2[b]
                u2[k, a + 1] = total if first_time else u2[k, a + 1] + total
                return inner

            return lax.fori_loop(0, na2, row, carry)

        lax.fori_loop(0, 3, one, 0)

    coarse_solve(True)

    def coarse_sweep(turn_number, carry):
        remainder(u2, 2, 0, na2, 1, ce, b2, 0, True)
        coarse_solve(False)
        return carry

    lax.fori_loop(0, 3, coarse_sweep, 0)

    for a in range(cq):
        for k in range(3):
            coarse_ref[a, k] = u2[k, pos * cq + a + 1, 0:cc, 0:rr]

    for i in range(cm + 2):
        for k in range(3):
            u1c[k, i] = u1b[k, i] + u2[k, pos * cq + (i + 1) // 2]
    whole_remainder(u1c, 1, cm, b1)
    correct(1, cm, u1c, u1d)
    edge_remainder(4, u1d, 1, cm, b1, pack1.at[4:6], got1.at[4:6])
    correct(1, cm, u1d, u1e)
    edge_start(5, u1e, cm, pack1.at[6:8], got1.at[6:8])
    edge_finish(5, u1e, cm, pack1.at[6:8], got1.at[6:8], True)

    for i in range(ca + 2):
        for k in range(3):
            u0c[k, i] = u0b[k, i] + u1e[k, (i + 1) // 2]
    whole_remainder(u0c, 0, ca, b0)
    correct(0, ca, u0c, u0d)
    edge_remainder(6, u0d, 0, ca, b0, pack0.at[4:6], got0.at[4:6])
    correct(0, ca, u0d, u0e)

    def solution_out():
        for k in range(3):
            sol_ref[:, k] = u0e[k, 1 : ca + 1, 0:cc, 0:rr]

    edge_remainder(7, u0e, 0, ca, b0, pack0.at[6:8], got0.at[6:8], False, solution_out)
    for k in range(3):
        res_ref[:, k] = rbuf[k, 0 : ca * cc, 0:rr].reshape(ca, cc, rr)


def body(load, region, family, stiffness, coupling, line_inverse, axial_inverse):
    nax, ncirc = lax.axis_size("ax"), lax.axis_size("circ")
    ca, cc, _, rr = load.shape
    lanes = -(-rr // 128) * 128
    ce = cc + 2 * DEEP
    cm, cq = ca // 2, ca // 4
    na2 = cq * nax
    rows = max(ca * cc, na2 * ce)
    rows1 = -(-3 * cm // 8) * 8
    vmem = pl.BlockSpec(memory_space=pltpu.VMEM)
    hbm = pl.BlockSpec(memory_space=pltpu.HBM)
    fine = pltpu.VMEM((3, ca + 2, ce, lanes), F32)
    mid = pltpu.VMEM((3, cm + 2, ce, lanes), F32)
    half = cq // 2
    sol, res, coarse = pl.pallas_call(
        functools.partial(kernel, (nax, ncirc, ca, cc, rr, lanes)),
        out_shape=[
            jax.ShapeDtypeStruct((ca, 3, cc, rr), F32),
            jax.ShapeDtypeStruct((ca, 3, cc, rr), F32),
            jax.ShapeDtypeStruct((cq, 3, cc, rr), F32),
        ],
        in_specs=[hbm] * 7,
        out_specs=[vmem, vmem, vmem],
        scratch_shapes=[
            pltpu.VMEM((ca, 3, cc, rr), F32),
            pltpu.VMEM((ca, cc, rr), jnp.int32),
            pltpu.VMEM((ca, cc, rr), jnp.int32),
            pltpu.SMEM((2, 3), F32),
            pltpu.SMEM((3, 2, 3), F32),
            pltpu.VMEM((9, rr, rr), F32),
            pltpu.SMEM((na2, na2), F32),
            pltpu.SemaphoreType.DMA((7,)),
        ]
        + [fine] * 6
        + [mid] * 6
        + [
            pltpu.VMEM((3, na2, ce, lanes), F32),
            pltpu.VMEM((2, na2, ce, lanes), F32),
            pltpu.VMEM((3, na2 + 2, ce, lanes), F32),
            pltpu.VMEM((na2, ce, lanes), F32),
            pltpu.VMEM((3, rows, lanes), F32),
            pltpu.VMEM((ca, cc, lanes), F32),
            pltpu.VMEM((ca, cc, lanes), F32),
            pltpu.VMEM((cm, cc, lanes), F32),
            pltpu.VMEM((cm, cc, lanes), F32),
            pltpu.VMEM((2, ca, lanes), F32),
            pltpu.VMEM((2, cm, lanes), F32),
            pltpu.VMEM((9, lanes, lanes), BF16),
            pltpu.VMEM((9, lanes, lanes), BF16),
            pltpu.VMEM((9, lanes, lanes), BF16),
            pltpu.VMEM((lanes, lanes), F32),
            pltpu.VMEM((8, 3 * ca, lanes), F32),
            pltpu.VMEM((8, 3 * ca, lanes), F32),
            pltpu.VMEM((8, rows1, lanes), F32),
            pltpu.VMEM((8, rows1, lanes), F32),
            pltpu.VMEM((2, 2, half, 8, lanes), F32),
            pltpu.VMEM((2, 2, half, 8, lanes), F32),
            pltpu.VMEM((2, 3, half, 8, lanes), F32),
            pltpu.VMEM((2, 3, half, 8, lanes), F32),
            pltpu.SemaphoreType.DMA((8, 4)),
            pltpu.SemaphoreType.DMA((8, 4)),
            pltpu.SemaphoreType.DMA((4, nax)),
            pltpu.SemaphoreType.DMA((4, nax)),
            pltpu.SemaphoreType.DMA((2, 2)),
            pltpu.SemaphoreType.DMA((2, 2)),
        ],
        compiler_params=pltpu.CompilerParams(
            collective_id=0, has_side_effects=True, vmem_limit_bytes=52 * 1024 * 1024
        ),
        name="vcycle",
    )(
        jnp.transpose(load, (0, 2, 1, 3)),
        region,
        family,
        stiffness,
        jnp.transpose(coupling, (1, 0, 2)),
        line_inverse.reshape(9, rr, rr),
        axial_inverse,
    )
    back = (0, 2, 1, 3)
    return jnp.transpose(sol, back), jnp.transpose(res, back), jnp.transpose(coarse, back)


def solution(mesh):
    field, cells = P("ax", "circ", None, None), P("ax", "circ", None)
    return jax.shard_map(
        body,
        mesh=mesh,
        in_specs=(field, cells, cells, P(), P(), P(), P()),
        out_specs=(field, field, field),
        check_vma=False,
    )
```

```python
import functools

import jax
import jax.numpy as jnp
from jax import lax
from jax.experimental import pallas as pl
from jax.experimental.pallas import tpu as pltpu
from jax.sharding import PartitionSpec as P

RADIAL_WEIGHT = 1024.0
DAMPING = 0.8
F32 = jnp.float32
BF16 = jnp.bfloat16
DEEP = 4


def kernel(
    dims,
    load_hbm,
    region_hbm,
    family_hbm,
    stiff_hbm,
    coup_hbm,
    inv_hbm,
    axial_hbm,
    sol_hbm,
    res_hbm,
    coarse_hbm,
    sol_ref,
    res_ref,
    coarse_ref,
    load_ref,
    region_ref,
    family_ref,
    stiff_ref,
    coup_ref,
    inv_ref,
    axial_ref,
    in_sem,
    out_sem,
    b0,
    u0a,
    u0b,
    u0c,
    u0d,
    u0e,
    b1,
    u1a,
    u1b,
    u1c,
    u1d,
    u1e,
    b2,
    c2,
    u2,
    y2,
    rbuf,
    reg0,
    sh0,
    reg1,
    sh1,
    ends0,
    ends1,
    wh,
    wm,
    wl,
    wtmp,
    pack0,
    got0,
    pack1,
    got1,
    packc,
    gotc,
    packb,
    gotb,
    send_sem,
    recv_sem,
    gsend,
    grecv,
    csend,
    crecv,
):
    nax, ncirc, ca, cc, rr, lanes = dims
    ce = cc + 2 * DEEP
    cm, cq = ca // 2, ca // 4
    na2 = cq * nax
    pos = lax.axis_index("ax")
    me_c = lax.axis_index("circ")
    ax_left, ax_right = lax.rem(pos + nax - 1, nax), lax.rem(pos + 1, nax)
    c_left, c_right = lax.rem(me_c + ncirc - 1, ncirc), lax.rem(me_c + 1, ncirc)
    has_left, has_right = pos > 0, pos < nax - 1

    arrivals = [
        pltpu.make_async_copy(source, target, in_sem.at[i])
        for i, (source, target) in enumerate(
            (
                (load_hbm, load_ref),
                (region_hbm, region_ref),
                (family_hbm, family_ref),
                (stiff_hbm, stiff_ref),
                (coup_hbm, coup_ref),
                (inv_hbm, inv_ref),
                (axial_hbm, axial_ref),
            )
        )
    ]
    for arrival in arrivals:
        arrival.start()

    departures = [
        pltpu.make_async_copy(source, target, out_sem.at[i])
        for i, (source, target) in enumerate(
            ((sol_ref, sol_hbm), (res_ref, res_hbm), (coarse_ref, coarse_hbm))
        )
    ]

    barrier = pltpu.get_barrier_semaphore()
    for d in range(1, nax):
        pl.semaphore_signal(barrier, inc=1, device_id=(lax.rem(pos + d, nax), me_c))
    pl.semaphore_signal(barrier, inc=1, device_id=(pos, c_left))
    pl.semaphore_signal(barrier, inc=1, device_id=(pos, c_right))

    b0[:, 1 : ca + 1, 0:cc, lanes - 128 : lanes] = jnp.zeros((3, ca, cc, 128), F32)
    arrivals[0].wait()
    for k in range(3):
        b0[k, 1 : ca + 1, 0:cc, 0:rr] = load_ref[:, k]

    def zero_row(buf, row):
        buf[:, row] = jnp.zeros((3, ce, lanes), F32)

    @pl.when(jnp.logical_not(has_left))
    def _():
        for buf in (b0, u0b, u1a, u1b, u1d, u1e, u0d, u0e):
            zero_row(buf, 0)

    @pl.when(jnp.logical_not(has_right))
    def _():
        for buf, row in (
            (b0, ca + 1),
            (u0b, ca + 1),
            (u0d, ca + 1),
            (u0e, ca + 1),
            (u1a, cm + 1),
            (u1b, cm + 1),
            (u1d, cm + 1),
            (u1e, cm + 1),
        ):
            zero_row(buf, row)

    zero_row(u2, 0)
    zero_row(u2, na2 + 1)

    def edge_copies(x, buf, rows, pack, got, k):
        def copy(source, target, sent, landed, to):
            return pltpu.make_async_remote_copy(
                src_ref=source,
                dst_ref=target,
                send_sem=send_sem.at[x, sent, k],
                recv_sem=recv_sem.at[x, landed, k],
                device_id=to,
            )

        left = copy(buf.at[k, 1, 0:cc], buf.at[k, rows + 1, 0:cc], 0, 1, (ax_left, me_c))
        right = copy(buf.at[k, rows, 0:cc], buf.at[k, 0, 0:cc], 1, 0, (ax_right, me_c))
        down = copy(pack.at[0, k], got.at[0, k], 2, 2, (pos, c_left))
        up = copy(pack.at[1, k], got.at[1, k], 3, 3, (pos, c_right))
        return left, right, down, up

    def edge_send(x, buf, rows, pack, got, k):
        left, right, down, up = edge_copies(x, buf, rows, pack, got, k)
        for a in range(rows):
            pack[0, k, a : a + 1, :] = buf[k, a + 1, 0:1, :]
            pack[1, k, a : a + 1, :] = buf[k, a + 1, cc - 1 : cc, :]
        down.start()
        up.start()

        @pl.when(has_left)
        def _():
            left.start()

        @pl.when(has_right)
        def _():
            right.start()

    def edge_finish(x, buf, rows, pack, got, keep=False):
        for k in range(3):
            left, right, down, up = edge_copies(x, buf, rows, pack, got, k)
            down.wait()
            up.wait()
            for a in range(rows if keep else 0):
                buf[k, a + 1, cc : cc + 1, :] = got[0, k, a : a + 1, :]
                buf[k, a + 1, ce - 1 : ce, :] = got[1, k, a : a + 1, :]

            @pl.when(has_left)
            def _():
                left.wait_send()
                right.wait_recv()

            @pl.when(has_right)
            def _():
                right.wait_send()
                left.wait_recv()

    mate = pos + 1 - 2 * lax.rem(pos, 2)

    def block_copy(which, slot, buf, cols, block, to):
        part = (slice(None), pl.ds(block * cq, cq), slice(*cols))
        return pltpu.make_async_remote_copy(
            src_ref=buf.at[part],
            dst_ref=buf.at[part],
            send_sem=gsend.at[which, slot],
            recv_sem=grecv.at[which, slot],
            device_id=(to, me_c),
        )

    def across(j):
        return lax.rem(pos + 2 * j, nax), lax.rem(pos + nax - 2 * j, nax)

    def gather_start(which, buf, cols):
        for j in range(1, nax // 2):
            block_copy(which, j, buf, cols, pos, across(j)[0]).start()
        block_copy(which, 0, buf, cols, pos, mate).start()

    def gather_forward(which, buf, cols):
        for j in range(1, nax // 2):
            block_copy(which, j, buf, cols, across(j)[1], across(j)[0]).wait_recv()
            block_copy(which, nax // 2 + j, buf, cols, across(j)[1], mate).start()

    def gather_finish(which, buf, cols):
        for j in range(1, nax // 2):
            block_copy(which, j, buf, cols, pos, across(j)[0]).wait_send()
            block_copy(which, nax // 2 + j, buf, cols, across(j)[1], mate).wait_send()
            theirs = lax.rem(mate + nax - 2 * j, nax)
            block_copy(which, nax // 2 + j, buf, cols, theirs, mate).wait_recv()
        block_copy(which, 0, buf, cols, pos, mate).wait_send()
        block_copy(which, 0, buf, cols, mate, mate).wait_recv()

    half = cq // 2
    base = pos * cq
    low = lax.broadcasted_iota(jnp.int32, (8, lanes), 0) < DEEP

    def turn(tile):
        return pltpu.roll(tile, DEEP, 0)

    def deep_copies(which, pack, got):
        return [
            pltpu.make_async_remote_copy(
                src_ref=pack.at[side],
                dst_ref=got.at[side],
                send_sem=csend.at[which, side],
                recv_sem=crecv.at[which, side],
                device_id=(pos, (c_left, c_right)[side]),
            )
            for side in range(2)
        ]

    def deep_start(which, buf, fields, pack, got):
        for f in range(fields):
            for a in range(half):
                pack[0, f, a] = jnp.where(low, buf[f, base + a, 0:8, :], turn(buf[f, base + a + half, 0:8, :]))
                pack[1, f, a] = jnp.where(
                    low,
                    turn(buf[f, base + a, cc - 8 : cc, :]),
                    buf[f, base + a + half, cc - 8 : cc, :],
                )
        for copy in deep_copies(which, pack, got):
            copy.start()

    def deep_finish(which, buf, fields, pack, got):
        for copy in deep_copies(which, pack, got):
            copy.wait()
        for f in range(fields):
            for a in range(half):
                right, left = got[0, f, a], got[1, f, a]
                buf[f, base + a, cc:ce, :] = jnp.where(low, right, turn(left))
                buf[f, base + a + half, cc:ce, :] = jnp.where(low, turn(right), left)

    def split(x):
        hi = x.astype(BF16)
        rest = x - hi.astype(F32)
        mid = rest.astype(BF16)
        return hi, mid, (rest - mid.astype(F32)).astype(BF16)

    def line(level, k, x):
        hi, mid, lo = split(x)
        i = level * 3 + k
        dot = functools.partial(jnp.dot, preferred_element_type=F32)
        small = dot(lo, wh[i]) + dot(hi, wl[i]) + dot(mid, wm[i])
        return dot(hi, wh[i]) + (dot(mid, wh[i]) + dot(hi, wm[i]) + small)

    arrivals[3].wait()
    arrivals[4].wait()
    stiff = [[stiff_ref[s, k] for k in range(3)] for s in range(2)]
    first = [[coup_ref[k, 0, e] for e in range(3)] for k in range(3)]
    diff = [[coup_ref[k, 1, e] - first[k][e] for e in range(3)] for k in range(3)]

    coefs = [(reg0, sh0), (reg1, sh1), (c2.at[0], c2.at[1])]
    edges = [ends0, ends1]

    def remainder(u, level, begin, count, stride, cols, rhs, shift, wrap):
        weight, (reg, share) = 0.25**level, coefs[level]
        gain = [stiff[1][k] - stiff[0][k] for k in range(3)]

        def row(step, carry):
            a = begin + step * stride
            own = [u[k, a + 1, 0:cols, :] for k in range(3)]
            region, fibre = reg[a, 0:cols, :], share[a, 0:cols, :]
            for k in range(3):
                c = own[k]
                if wrap:
                    around = pltpu.roll(c, 1, 0) + pltpu.roll(c, cols - 1, 0)
                else:
                    wide = u[k, a + 1]
                    around = pltpu.roll(wide, 1, 0)[0:cols] + pltpu.roll(wide, ce - 1, 0)[0:cols]
                beside = pltpu.roll(c, 1, 1) + pltpu.roll(c, lanes - 1, 1)
                axial = u[k, a, 0:cols, :] + u[k, a + 2, 0:cols, :]
                lap = (
                    (2.0 * weight + 2.0 + 2.0 * RADIAL_WEIGHT) * c
                    - weight * axial
                    - around
                    - RADIAL_WEIGHT * beside
                )
                mix = own[0] * first[k][0] + own[1] * first[k][1] + own[2] * first[k][2]
                more = own[0] * diff[k][0] + own[1] * diff[k][1] + own[2] * diff[k][2]
                value = (stiff[0][k] + region * gain[k]) * lap + (c + mix + fibre * more)
                rbuf[k, pl.ds(pl.multiple_of(a * cols, 8), cols), :] = (
                    rhs[k, a + shift, 0:cols, :] - value
                )
            return carry

        lax.fori_loop(0, count, row, 0)

    def whole_remainder(u, level, rows, rhs):
        remainder(u, level, 0, rows, 1, cc, rhs, 1, False)

    def side_columns(level, rows, changes):
        ends = edges[level]
        for k in range(3):
            for side, col in ((0, cc - 1), (1, 0)):
                coef = stiff[0][k] + ends[side, 0:rows, :] * (stiff[1][k] - stiff[0][k])
                parts = [(got[side, k] - pack[side, k], times) for pack, got, times in changes]
                for a in range(rows):
                    place = a * cc + col
                    more = sum(part[a // times : a // times + 1] for part, times in parts)
                    rbuf[k, place : place + 1, :] = (
                        rbuf[k, place : place + 1, :] + coef[a : a + 1] * more
                    )

    def edge_remainder(x, u, level, rows, rhs, pack, got, keep=False, between=None):
        remainder(u, level, 1, rows - 2, 1, cc, rhs, 1, True)
        if between is not None:
            between()
        edge_finish(x, u, rows, pack, got, keep)
        remainder(u, level, 0, 2, rows - 1, cc, rhs, 1, True)
        side_columns(level, rows, [(pack, got, 1)])

    def correct(level, rows, old, new, x, pack, got):
        def one(k, carry):
            step = line(level, k, rbuf[k, 0 : rows * cc, :]).reshape(rows, cc, lanes)
            new[k, 1 : rows + 1, 0:cc, :] = old[k, 1 : rows + 1, 0:cc, :] + step
            edge_send(x, new, rows, pack, got, k)
            return carry

        lax.fori_loop(0, 3, one, 0)

    def first_sweep(level, rhs, rows, new):
        def one(k, carry):
            step = line(level, k, rhs[k].reshape(rows * ce, lanes))
            new[k] = step.reshape(rows, ce, lanes)
            return carry

        lax.fori_loop(0, 3, one, 0)

    def start_from(level, rhs, rows, new, x, pack, got):
        def one(k, carry):
            step = line(level, k, rhs[k, 1 : rows + 1, 0:cc, :].reshape(rows * cc, lanes))
            new[k, 1 : rows + 1, 0:cc, :] = step.reshape(rows, cc, lanes)
            edge_send(x, new, rows, pack, got, k)
            return carry

        lax.fori_loop(0, 3, one, 0)

    def restrict_into(rows, write):
        for k in range(3):
            r = rbuf[k, 0 : rows * cc, :].reshape(rows // 2, 2, cc, lanes)
            write(k, 0.5 * (r[:, 0] + r[:, 1]))

    pl.semaphore_wait(barrier, nax + 1)
    for k in range(3):
        edge_send(0, b0, ca, pack0, got0, k)

    zeros = jnp.zeros((ca, cc, lanes), F32)
    arrivals[1].wait()
    arrivals[2].wait()
    reg0[...] = zeros
    sh0[...] = zeros
    reg0[:, :, 0:rr] = jnp.where(region_ref[...] == 0, 0.0, 1.0)
    sh0[:, :, 0:rr] = jnp.where(family_ref[...] == 1, 1.0, 0.0)
    for fine_c, mid_c, f in ((reg0, reg1, 0), (sh0, sh1, 1)):
        for a in range(cm):
            mid_c[a] = 0.5 * (fine_c[2 * a] + fine_c[2 * a + 1])
        for a in range(cq):
            c2[f, pos * cq + a, 0:cc, :] = 0.5 * (mid_c[2 * a] + mid_c[2 * a + 1])
    gather_start(0, c2, (0, cc))
    deep_start(0, c2, 2, packc, gotc)
    for ends, reg, rows in ((ends0, reg0, ca), (ends1, reg1, cm)):
        for a in range(rows):
            ends[0, a : a + 1, :] = reg[a, cc - 1 : cc, :]
            ends[1, a : a + 1, :] = reg[a, 0:1, :]

    arrivals[5].wait()
    arrivals[6].wait()
    wtmp[...] = jnp.zeros((lanes, lanes), F32)

    def prepare(i, carry):
        wtmp[0:rr, 0:rr] = inv_ref[i] * DAMPING
        wh[i], wm[i], wl[i] = split(jnp.transpose(wtmp[...]))
        return carry

    lax.fori_loop(0, 9, prepare, 0)

    edge_finish(0, b0, ca, pack0, got0, True)
    first_sweep(0, b0, ca + 2, u0a)
    whole_remainder(u0a, 0, ca, b0)
    correct(0, ca, u0a, u0b, 1, pack0.at[2:4], got0.at[2:4])

    def coefficients_on():
        deep_finish(0, c2, 2, packc, gotc)
        gather_start(1, c2, (cc, ce))
        gather_forward(0, c2, (0, cc))
        gather_finish(0, c2, (0, cc))

    edge_remainder(1, u0b, 0, ca, b0, pack0.at[2:4], got0.at[2:4], False, coefficients_on)

    def into_b1(k, value):
        b1[k, 1 : cm + 1, 0:cc, :] = value

    restrict_into(ca, into_b1)

    start_from(1, b1, cm, u1a, 2, pack1, got1)
    edge_remainder(2, u1a, 1, cm, b1, pack1, got1)
    correct(1, cm, u1a, u1b, 3, pack1.at[2:4], got1.at[2:4])
    edge_remainder(3, u1b, 1, cm, b1, pack1.at[2:4], got1.at[2:4], True)

    def into_b2(k, value):
        b2[k, pl.ds(pos * cq, cq), 0:cc, :] = value

    restrict_into(cm, into_b2)

    deep_start(1, b2, 3, packb, gotb)
    gather_start(2, b2, (0, cc))
    gather_forward(1, c2, (cc, ce))
    gather_finish(1, c2, (cc, ce))
    gather_forward(2, b2, (0, cc))
    deep_finish(1, b2, 3, packb, gotb)
    gather_start(3, b2, (cc, ce))
    gather_forward(3, b2, (cc, ce))
    gather_finish(2, b2, (0, cc))
    gather_finish(3, b2, (cc, ce))

    def coarse_solve(first_time):
        def one(k, carry):
            x = b2[k].reshape(na2 * ce, lanes) if first_time else rbuf[k, 0 : na2 * ce, :]
            y2[...] = line(2, k, x).reshape(na2, ce, lanes)

            def row(a, inner):
                total = axial_ref[a, 0] * y2[0]
                for b in range(1, na2):
                    total = total + axial_ref[a, b] * y2[b]
                u2[k, a + 1] = total if first_time else u2[k, a + 1] + total
                return inner

            return lax.fori_loop(0, na2, row, carry)

        lax.fori_loop(0, 3, one, 0)

    coarse_solve(True)

    def coarse_sweep(turn_number, carry):
        remainder(u2, 2, 0, na2, 1, ce, b2, 0, True)
        coarse_solve(False)
        return carry

    lax.fori_loop(0, 3, coarse_sweep, 0)

    for a in range(cq):
        for k in range(3):
            coarse_ref[a, k] = u2[k, pos * cq + a + 1, 0:cc, 0:rr]
    departures[2].start()

    for i in range(cm + 2):
        for k in range(3):
            u1c[k, i] = u1b[k, i] + u2[k, pos * cq + (i + 1) // 2]
    whole_remainder(u1c, 1, cm, b1)
    correct(1, cm, u1c, u1d, 4, pack1.at[4:6], got1.at[4:6])
    edge_remainder(4, u1d, 1, cm, b1, pack1.at[4:6], got1.at[4:6])
    correct(1, cm, u1d, u1e, 5, pack1.at[6:8], got1.at[6:8])

    def lift(i):
        for k in range(3):
            u0c[k, i, 0:cc, :] = u0b[k, i, 0:cc, :] + u1e[k, (i + 1) // 2, 0:cc, :]

    for i in range(1, ca + 1):
        lift(i)
    remainder(u0c, 0, 1, ca - 2, 1, cc, b0, 1, True)
    edge_finish(5, u1e, cm, pack1.at[6:8], got1.at[6:8])
    lift(0)
    lift(ca + 1)
    remainder(u0c, 0, 0, 2, ca - 1, cc, b0, 1, True)
    side_columns(
        0,
        ca,
        [(pack0.at[2:4], got0.at[2:4], 1), (pack1.at[6:8], got1.at[6:8], 2)],
    )
    correct(0, ca, u0c, u0d, 6, pack0.at[4:6], got0.at[4:6])
    edge_remainder(6, u0d, 0, ca, b0, pack0.at[4:6], got0.at[4:6])
    correct(0, ca, u0d, u0e, 7, pack0.at[6:8], got0.at[6:8])

    def solution_out():
        for k in range(3):
            sol_ref[:, k] = u0e[k, 1 : ca + 1, 0:cc, 0:rr]
        departures[0].start()

    edge_remainder(7, u0e, 0, ca, b0, pack0.at[6:8], got0.at[6:8], False, solution_out)
    for k in range(3):
        res_ref[:, k] = rbuf[k, 0 : ca * cc, 0:rr].reshape(ca, cc, rr)
    departures[1].start()
    for departure in departures:
        departure.wait()


def body(load, region, family, stiffness, coupling, line_inverse, axial_inverse):
    nax, ncirc = lax.axis_size("ax"), lax.axis_size("circ")
    ca, cc, _, rr = load.shape
    lanes = -(-rr // 128) * 128
    ce = cc + 2 * DEEP
    cm, cq = ca // 2, ca // 4
    na2 = cq * nax
    rows = max(ca * cc, na2 * ce)
    hbm = pl.BlockSpec(memory_space=pltpu.HBM)
    fine = pltpu.VMEM((3, ca + 2, ce, lanes), F32)
    mid = pltpu.VMEM((3, cm + 2, ce, lanes), F32)
    half = cq // 2
    sol, res, coarse = pl.pallas_call(
        functools.partial(kernel, (nax, ncirc, ca, cc, rr, lanes)),
        out_shape=[
            jax.ShapeDtypeStruct((ca, 3, cc, rr), F32),
            jax.ShapeDtypeStruct((ca, 3, cc, rr), F32),
            jax.ShapeDtypeStruct((cq, 3, cc, rr), F32),
        ],
        in_specs=[hbm] * 7,
        out_specs=[hbm] * 3,
        scratch_shapes=[
            pltpu.VMEM((ca, 3, cc, rr), F32),
            pltpu.VMEM((ca, 3, cc, rr), F32),
            pltpu.VMEM((cq, 3, cc, rr), F32),
            pltpu.VMEM((ca, 3, cc, rr), F32),
            pltpu.VMEM((ca, cc, rr), jnp.int32),
            pltpu.VMEM((ca, cc, rr), jnp.int32),
            pltpu.SMEM((2, 3), F32),
            pltpu.SMEM((3, 2, 3), F32),
            pltpu.VMEM((9, rr, rr), F32),
            pltpu.SMEM((na2, na2), F32),
            pltpu.SemaphoreType.DMA((7,)),
            pltpu.SemaphoreType.DMA((3,)),
        ]
        + [fine] * 6
        + [mid] * 6
        + [
            pltpu.VMEM((3, na2, ce, lanes), F32),
            pltpu.VMEM((2, na2, ce, lanes), F32),
            pltpu.VMEM((3, na2 + 2, ce, lanes), F32),
            pltpu.VMEM((na2, ce, lanes), F32),
            pltpu.VMEM((3, rows, lanes), F32),
            pltpu.VMEM((ca, cc, lanes), F32),
            pltpu.VMEM((ca, cc, lanes), F32),
            pltpu.VMEM((cm, cc, lanes), F32),
            pltpu.VMEM((cm, cc, lanes), F32),
            pltpu.VMEM((2, ca, lanes), F32),
            pltpu.VMEM((2, cm, lanes), F32),
            pltpu.VMEM((9, lanes, lanes), BF16),
            pltpu.VMEM((9, lanes, lanes), BF16),
            pltpu.VMEM((9, lanes, lanes), BF16),
            pltpu.VMEM((lanes, lanes), F32),
            pltpu.VMEM((8, 3, ca, lanes), F32),
            pltpu.VMEM((8, 3, ca, lanes), F32),
            pltpu.VMEM((8, 3, cm, lanes), F32),
            pltpu.VMEM((8, 3, cm, lanes), F32),
            pltpu.VMEM((2, 2, half, 8, lanes), F32),
            pltpu.VMEM((2, 2, half, 8, lanes), F32),
            pltpu.VMEM((2, 3, half, 8, lanes), F32),
            pltpu.VMEM((2, 3, half, 8, lanes), F32),
            pltpu.SemaphoreType.DMA((8, 4, 3)),
            pltpu.SemaphoreType.DMA((8, 4, 3)),
            pltpu.SemaphoreType.DMA((4, nax)),
            pltpu.SemaphoreType.DMA((4, nax)),
            pltpu.SemaphoreType.DMA((2, 2)),
            pltpu.SemaphoreType.DMA((2, 2)),
        ],
        compiler_params=pltpu.CompilerParams(
            collective_id=0, has_side_effects=True, vmem_limit_bytes=63 * 1024 * 1024
        ),
        name="vcycle",
    )(
        jnp.transpose(load, (0, 2, 1, 3)),
        region,
        family,
        stiffness,
        jnp.transpose(coupling, (1, 0, 2)),
        line_inverse.reshape(9, rr, rr),
        axial_inverse,
    )
    back = (0, 2, 1, 3)
    return jnp.transpose(sol, back), jnp.transpose(res, back), jnp.transpose(coarse, back)


def solution(mesh):
    field, cells = P("ax", "circ", None, None), P("ax", "circ", None)
    return jax.shard_map(
        body,
        mesh=mesh,
        in_specs=(field, cells, cells, P(), P(), P(), P()),
        out_specs=(field, field, field),
        check_vma=False,
    )
```
